128 devices in a mesh: tile: 32 (over z, x, y_lo), lev: 4 (over y_hi, core).
Axes of the slice: x: 4, y: 4 (y_hi: 2, y_lo: 2; y = y_hi * 2 + y_lo), z: 4, core: 2. Of those that a mesh axis runs over, the one named last changes fastest.
Arguments:
- ensemble: bfloat16 [80, 4194304], P(None, ('tile', 'lev')), may hold values from -6 to 6
- obs_pert: bfloat16 [80, 2097152], P(None, ('tile', 'lev')), may hold values from -4 to 4
- innovation: float32 [2097152], P(('tile', 'lev')), may hold values from -12 to 12
- obs_rinv: float32 [2097152], P(('tile', 'lev')), may hold values from 0.25 to 4
- loc_weight: float32 [3, 2097152], P(None, ('tile', 'lev')), may hold values from 0.05 to 1
- obs_count: int32 [128], P(('tile', 'lev')), may hold values from 4096 to 16384, as said below
Outputs:
- analysis: bfloat16 [80, 4194304], P(None, ('tile', 'lev'))
The draws below stay inside these ranges and needn't reach their ends.
Inputs may be any that keep to these rules, and one draw needn't show every extreme that they name: `obs_count`: some block has all 16384 slots valid in every draw.
All inputs are finite; a program needn't handle non-finite values.
Results may differ from the reference program's by a relative error of at most 0.007.
Values may be sent and summed in bfloat16 or wider, within the bound.
No kernel may reach another device: no remote copies, remote signals or barrier semaphores. Data moves between devices by JAX's collectives and lax.ppermute only.
A program may use at most 64 MiB of HBM per device.

```python
import math
import jax
import jax.numpy as jnp
from jax import lax

K = 80
OBS_DEV = 16384
COL_DEV = 32768
NS_STEPS = 10
BLOCKS = 128
NOBS = 2097152
NCOL = 4194304
N_TILE = 32
N_LEV = 4


def draw_obs_count(key, part):
    key = jax.random.fold_in(key, 7)
    first, second = jax.random.split(key)
    counts = jax.random.randint(first, (BLOCKS,), OBS_DEV // 4, OBS_DEV + 1)
    where = jax.random.randint(second, (), 0, BLOCKS)
    return counts.at[where].set(OBS_DEV).astype(jnp.int32)


def steps_of(rng, dims, cuts, least, largest):
    gain = 1.0
    for position, blocks in cuts:
        heights = jax.random.uniform(jax.random.fold_in(jax.random.fold_in(rng, 6), position), (blocks,), jnp.float32, least / len(cuts), largest / len(cuts))
        gain = gain * jnp.repeat(jnp.exp(heights), dims[position] // blocks).reshape((-1,) + (1,) * (len(dims) - 1 - position))
    return gain


def normal_values(own_key, dims, deviation, limit, shards=(), held_as=jnp.bfloat16):
    level = steps_of(own_key, dims, shards, -0.22, 0.18) if shards else 1.0
    array = jax.random.normal(own_key, dims, jnp.float32) * deviation * level
    return jnp.minimum(jnp.maximum(array, -limit), limit).astype(held_as)


def setup_inputs(seed: int = 0) -> dict:
    keys = jax.random.split(jax.random.key(seed), 7)
    ensemble = normal_values(keys[0], (K, NCOL), 1.0, 6.0, ((1, 128),))
    obs_pert = normal_values(keys[1], (K, NOBS), 0.5, 4.0, ((1, 128),))
    innovation = normal_values(keys[2], (NOBS,), 2.0, 12.0, ((0, 128),), jnp.float32)
    obs_rinv = jnp.clip(jnp.exp(math.log(4.0) - 2.7725887 * jax.random.uniform(keys[3], (NOBS,), jnp.float32) ** steps_of(keys[3], (NOBS,), ((0, 128),), -0.2, 0.2)), 0.25, 4.0)
    loc_weight = jnp.clip(0.05 + 0.95 * jax.random.uniform(keys[4], (3, NOBS), jnp.float32) ** steps_of(keys[4], (3, NOBS), ((1, 128),), -0.2, 0.2), 0.05, 1.0)
    obs_count = draw_obs_count(jax.random.fold_in(keys[6], 71), 0)
    return dict(ensemble=ensemble, obs_pert=obs_pert, innovation=innovation, obs_rinv=obs_rinv, loc_weight=loc_weight, obs_count=obs_count)


def weighted_gram(pert, innov, weight):
    root = jnp.sqrt(weight)
    ext = (jnp.concatenate([pert.astype(jnp.float32), innov[None, :]], axis=0) * root[None, :]).astype(jnp.bfloat16)
    return jnp.dot(ext, ext.T, preferred_element_type=jnp.float32)

def analyse(gram, ensemble):
    members = ensemble.shape[0]
    cov = gram[:members, :members]
    proj = gram[:members, members]
    eye = jnp.eye(members, dtype=jnp.float32)
    mat = (members - 1.0) * eye + cov
    scale = jnp.sqrt(jnp.sum(mat * mat))
    iterate = mat / scale
    inverse_root = eye
    for step in range(NS_STEPS):
        factor = 1.5 * eye - 0.5 * jnp.dot(inverse_root, iterate, precision=lax.Precision.HIGHEST)
        iterate = jnp.dot(iterate, factor, precision=lax.Precision.HIGHEST)
        inverse_root = jnp.dot(factor, inverse_root, precision=lax.Precision.HIGHEST)
    root_inv = inverse_root / jnp.sqrt(scale)
    precision_mat = jnp.dot(root_inv, root_inv, precision=lax.Precision.HIGHEST)
    mean_weight = jnp.dot(precision_mat, proj, precision=lax.Precision.HIGHEST)
    transform = (jnp.sqrt(members - 1.0) * root_inv + mean_weight[:, None]).astype(jnp.bfloat16)
    mean_state = lax.optimization_barrier(jnp.mean(ensemble.astype(jnp.float32), axis=0))
    keep = 1.0 - lax.optimization_barrier(jnp.sum(transform.astype(jnp.float32), axis=0))
    result = jnp.dot(transform.T, ensemble, preferred_element_type=jnp.float32) + keep[:, None] * mean_state[None, :]
    return result.astype(jnp.bfloat16)

def reference(ensemble, obs_pert, innovation, obs_rinv, loc_weight, obs_count):
    slots = jnp.arange(NOBS, dtype=jnp.int32)
    live = (slots % OBS_DEV < jnp.repeat(obs_count, OBS_DEV)).astype(jnp.float32)
    side = jnp.stack([innovation, obs_rinv * loc_weight[0] * live, obs_rinv * loc_weight[1] * live, obs_rinv * loc_weight[2] * live]).astype(jnp.bfloat16)
    side32 = side.astype(jnp.float32)
    span = OBS_DEV * N_LEV
    cols = COL_DEV * N_LEV

    def one_tile(t, out):
        total = jnp.zeros((K + 1, K + 1), jnp.float32)
        for offset, row in ((-1, 3), (0, 2), (1, 1)):
            src = ((t + offset + N_TILE) % N_TILE).astype(jnp.int32)
            start = (src * span).astype(jnp.int32)
            pert = lax.dynamic_slice_in_dim(obs_pert, start, span, 1)
            innov = lax.dynamic_slice_in_dim(side32[0], start, span, 0)
            weight = lax.dynamic_slice_in_dim(side32[row], start, span, 0)
            total = total + weighted_gram(pert, innov, weight)
        cstart = (t * cols).astype(jnp.int32)
        block = lax.dynamic_slice_in_dim(ensemble, cstart, cols, 1)
        return lax.dynamic_update_slice_in_dim(out, analyse(total, block), cstart, 1)
    return lax.fori_loop(0, N_TILE, one_tile, jnp.zeros((K, NCOL), jnp.bfloat16))
```

```python
import functools
import math

import jax
import jax.numpy as jnp
from jax import lax
from jax.experimental import pallas as pl
from jax.experimental.pallas import tpu as pltpu
from jax.sharding import PartitionSpec as P

NS_STEPS = 10
GRAM_CHUNKS = 4
COPY_CHUNKS = 8
PIECE = 1024
VMEM_BYTES = 40 * 1024 * 1024


def gram_kernel(info, pert, innov, rinv, loc, out):
    step = pl.program_id(0)
    members, width = pert.shape
    slots = step * width + lax.broadcasted_iota(jnp.int32, (1, width), 1)
    live = (slots < info[0]).astype(jnp.float32)
    even = info[1] == 0
    scaled = rinv[...]
    before, own, after = [
        (scaled * loc[i : i + 1, :] * live).astype(jnp.bfloat16) for i in range(3)
    ]
    near = jnp.where(even, after, before)
    far = jnp.where(even, before, after)
    block = pert[...]
    right = jnp.concatenate(
        [block, jnp.broadcast_to(innov[...].astype(jnp.bfloat16), (16, width))], axis=0
    )
    left = jnp.concatenate([block * far, block * near, block * own], axis=0)
    gram = lax.dot_general(left, right, (((1,), (1,)), ((), ())), preferred_element_type=jnp.float32)

    @pl.when(step == 0)
    def _():
        out[...] = jnp.zeros_like(out)

    out[:, : members + 16] += gram


def grams(pert, innov, rinv, loc, info):
    members, width = pert.shape
    chunk = width // GRAM_CHUNKS
    return pl.pallas_call(
        gram_kernel,
        grid=(GRAM_CHUNKS,),
        in_specs=[
            pl.BlockSpec(memory_space=pltpu.SMEM),
            pl.BlockSpec((members, chunk), lambda i: (0, i)),
            pl.BlockSpec((1, chunk), lambda i: (0, i)),
            pl.BlockSpec((1, chunk), lambda i: (0, i)),
            pl.BlockSpec((3, chunk), lambda i: (0, i)),
        ],
        out_specs=pl.BlockSpec((3 * members, 128), lambda i: (0, 0)),
        out_shape=jax.ShapeDtypeStruct((3 * members, 128), jnp.float32),
        compiler_params=pltpu.CompilerParams(vmem_limit_bytes=VMEM_BYTES),
        name="grams",
    )(info, pert, innov, rinv, loc)


def exact(a, b):
    return jnp.dot(a, b, precision=lax.Precision.HIGHEST, preferred_element_type=jnp.float32)


def transform_of(total):
    members = total.shape[0]
    rows = lax.broadcasted_iota(jnp.int32, total.shape, 0)
    cols = lax.broadcasted_iota(jnp.int32, total.shape, 1)
    eye = (rows == cols).astype(jnp.float32)[:, :members]
    mat = (members - 1.0) * eye + total[:, :members]
    scale = jnp.sqrt(jnp.sum(mat * mat))
    iterate = mat / scale
    factor = 1.5 * eye - 0.5 * iterate
    inverse_root = factor
    iterate = exact(iterate, factor)
    for _ in range(NS_STEPS - 1):
        factor = 1.5 * eye - 0.5 * exact(inverse_root, iterate)
        iterate = exact(iterate, factor)
        inverse_root = exact(factor, inverse_root)
    root_inv = inverse_root / jnp.sqrt(scale)
    mean_weight = exact(root_inv, exact(root_inv, total))[:, members : members + 1]
    transform = (math.sqrt(members - 1.0) * root_inv + mean_weight).astype(jnp.bfloat16)
    flipped = transform.astype(jnp.float32).T
    keep = 1.0 - jnp.sum(flipped, axis=1, keepdims=True)
    return flipped + keep / members


def analysis_kernel(own, other, mine, theirs, ensemble, out, held, result, left, in_sem, out_sem):
    members, width = held.shape
    chunk = width // COPY_CHUNKS

    def fetch(i):
        part = pl.ds(i * chunk, chunk)
        return pltpu.make_async_copy(ensemble.at[:, part], held.at[:, part], in_sem.at[i])

    def store(i):
        part = pl.ds(i * chunk, chunk)
        return pltpu.make_async_copy(result.at[:, part], out.at[:, part], out_sem.at[i])

    for i in range(COPY_CHUNKS):
        fetch(i).start()
    weights = transform_of(own[...] + other[...] + mine[...] + theirs[...])
    high = weights.astype(jnp.bfloat16)
    low = (weights - high.astype(jnp.float32)).astype(jnp.bfloat16)
    left[...] = jnp.concatenate([high, low], axis=1)

    for i in range(COPY_CHUNKS):
        fetch(i).wait()

        @pl.loop(0, chunk // PIECE)
        def _(j):
            part = pl.ds(pl.multiple_of(i * chunk + j * PIECE, PIECE), PIECE)
            block = held[:, part]
            both = jnp.concatenate([block, block], axis=0)
            result[:, part] = jnp.dot(
                left[...], both, preferred_element_type=jnp.float32
            ).astype(jnp.bfloat16)

        store(i).start()
    for i in range(COPY_CHUNKS):
        store(i).wait()


def analysis(own, other, mine, theirs, ensemble):
    members, width = ensemble.shape
    small = pl.BlockSpec(memory_space=pltpu.VMEM)
    return pl.pallas_call(
        analysis_kernel,
        in_specs=[small] * 4 + [pl.BlockSpec(memory_space=pl.ANY)],
        out_specs=pl.BlockSpec(memory_space=pl.ANY),
        out_shape=jax.ShapeDtypeStruct((members, width), jnp.bfloat16),
        scratch_shapes=[
            pltpu.VMEM((members, width), jnp.bfloat16),
            pltpu.VMEM((members, width), jnp.bfloat16),
            pltpu.VMEM((members, 2 * members), jnp.bfloat16),
            pltpu.SemaphoreType.DMA((COPY_CHUNKS,)),
            pltpu.SemaphoreType.DMA((COPY_CHUNKS,)),
        ],
        compiler_params=pltpu.CompilerParams(vmem_limit_bytes=VMEM_BYTES),
        name="analysis",
    )(own, other, mine, theirs, ensemble)


def local(n_tile, n_lev, ensemble, obs_pert, innovation, obs_rinv, loc_weight, obs_count):
    members = obs_pert.shape[0]
    axes = ("tile", "lev")

    def pairs(partner):
        return [
            (t * n_lev + l, (lambda a, b: a * n_lev + b)(*partner(t, l)))
            for t in range(n_tile)
            for l in range(n_lev)
        ]

    core = pairs(lambda t, l: (t, l ^ 1))
    high = pairs(lambda t, l: (t, l ^ 2))
    near = pairs(lambda t, l: (t ^ 1, l ^ (2 * (l & 1))))
    far = pairs(lambda t, l: ((t + 1 if t & 1 else t - 1) % n_tile, l ^ (2 * (l & 1))))

    parity = lax.rem(lax.axis_index("tile"), 2).astype(jnp.int32)
    info = jnp.concatenate([obs_count, parity[None]])
    gram = grams(obs_pert, innovation[None, :], obs_rinv[None, :], loc_weight, info)
    gram = gram + lax.ppermute(gram, axes, core)
    to_far, to_near, own = gram[:members], gram[members : 2 * members], gram[2 * members :]
    from_far = lax.ppermute(to_far, axes, far)
    from_near = lax.ppermute(to_near, axes, near)
    other = lax.ppermute(own, axes, high)
    mine = from_far + from_near
    theirs = lax.ppermute(mine, axes, core)
    return analysis(own, other, mine, theirs, ensemble)


def solution(mesh):
    return jax.shard_map(
        functools.partial(local, mesh.shape["tile"], mesh.shape["lev"]),
        mesh=mesh,
        in_specs=(
            P(None, ("tile", "lev")),
            P(None, ("tile", "lev")),
            P(("tile", "lev")),
            P(("tile", "lev")),
            P(None, ("tile", "lev")),
            P(("tile", "lev")),
        ),
        out_specs=P(None, ("tile", "lev")),
        check_vma=False,
    )
```

```python
import functools
import math

import jax
import jax.numpy as jnp
from jax import lax
from jax.experimental import pallas as pl
from jax.experimental.pallas import tpu as pltpu
from jax.sharding import PartitionSpec as P

NS_STEPS = 10
OBS_CHUNKS = 2
FETCHES = 4
STORES = (2048, 2048, 4096, 8192, 8192, 4096, 2048, 2048)
VMEM_BYTES = 40 * 1024 * 1024


def in_hbm(array):
    return pltpu.with_memory_space_constraint(array, pltpu.HBM)


def gram_kernel(
    count, parity, pert, innov, rinv, loc, out, pert_in, innov_in, rinv_in, loc_in, pert_sem, sem
):
    members, width = pert_in.shape
    chunk = width // OBS_CHUNKS
    sides = [
        pltpu.make_async_copy(source, target, sem.at[i])
        for i, (source, target) in enumerate(((rinv, rinv_in), (loc, loc_in), (innov, innov_in)))
    ]
    blocks = []
    for i in range(OBS_CHUNKS):
        part = pl.ds(i * chunk, chunk)
        blocks.append(pltpu.make_async_copy(pert.at[:, part], pert_in.at[:, part], pert_sem.at[i]))
    for copy in sides + blocks:
        copy.start()
    for copy in sides:
        copy.wait()
    even = parity[0] == 0
    total = None
    for i in range(OBS_CHUNKS):
        part = pl.ds(i * chunk, chunk)
        slots = i * chunk + lax.broadcasted_iota(jnp.int32, (1, chunk), 1)
        live = (slots < count[0]).astype(jnp.float32)
        scaled = rinv_in[:, part]
        before, own, after = [
            (scaled * loc_in[j : j + 1, part] * live).astype(jnp.bfloat16) for j in range(3)
        ]
        near = jnp.where(even, after, before)
        far = jnp.where(even, before, after)
        side = jnp.broadcast_to(innov_in[:, part].astype(jnp.bfloat16), (16, chunk))
        blocks[i].wait()
        block = pert_in[:, part]
        left = jnp.concatenate([block * far, block * near, block * own], axis=0)
        right = jnp.concatenate([block, side], axis=0)
        gram = lax.dot_general(
            left, right, (((1,), (1,)), ((), ())), preferred_element_type=jnp.float32
        )
        total = gram if total is None else total + gram
    out[:, : members + 16] = total
    out[:, members + 16 :] = jnp.zeros((3 * members, 112 - members), jnp.float32)


def grams(pert, innov, rinv, loc, count, parity):
    members, width = pert.shape
    return pl.pallas_call(
        gram_kernel,
        in_specs=[pl.BlockSpec(memory_space=pltpu.SMEM)] * 2
        + [pl.BlockSpec(memory_space=pltpu.HBM)] * 4,
        out_specs=pl.BlockSpec(memory_space=pltpu.VMEM),
        out_shape=jax.ShapeDtypeStruct((3 * members, 128), jnp.float32),
        scratch_shapes=[
            pltpu.VMEM((members, width), jnp.bfloat16),
            pltpu.VMEM((1, width), jnp.float32),
            pltpu.VMEM((1, width), jnp.float32),
            pltpu.VMEM((3, width), jnp.float32),
            pltpu.SemaphoreType.DMA((OBS_CHUNKS,)),
            pltpu.SemaphoreType.DMA((3,)),
        ],
        compiler_params=pltpu.CompilerParams(vmem_limit_bytes=VMEM_BYTES),
        name="grams",
    )(count, parity, *(in_hbm(x) for x in (pert, innov, rinv, loc)))


def exact(a, b):
    return jnp.dot(a, b, precision=lax.Precision.HIGHEST, preferred_element_type=jnp.float32)


def transform_of(total):
    members = total.shape[0]
    rows = lax.broadcasted_iota(jnp.int32, total.shape, 0)
    cols = lax.broadcasted_iota(jnp.int32, total.shape, 1)
    eye = (rows == cols).astype(jnp.float32)[:, :members]
    mat = (members - 1.0) * eye + total[:, :members]
    scale = jnp.sqrt(jnp.sum(mat * mat))
    iterate = mat / scale
    factor = 1.5 * eye - 0.5 * iterate
    inverse_root = factor
    iterate = exact(iterate, factor)
    for _ in range(NS_STEPS - 1):
        factor = 1.5 * eye - 0.5 * exact(inverse_root, iterate)
        iterate = exact(iterate, factor)
        inverse_root = exact(factor, inverse_root)
    root_inv = inverse_root / jnp.sqrt(scale)
    mean_weight = exact(root_inv, exact(root_inv, total))[:, members : members + 1]
    transform = (math.sqrt(members - 1.0) * root_inv + mean_weight).astype(jnp.bfloat16)
    flipped = transform.astype(jnp.float32).T
    keep = 1.0 - jnp.sum(flipped, axis=1, keepdims=True)
    return flipped + keep / members


def analysis_kernel(own, other, mine, theirs, ensemble, out, held, result, in_sem, out_sem):
    members, width = held.shape
    chunk = width // FETCHES
    fetches, stores, parts = [], [], []
    for i in range(FETCHES):
        part = pl.ds(i * chunk, chunk)
        fetches.append(pltpu.make_async_copy(ensemble.at[:, part], held.at[:, part], in_sem.at[i]))
    for i, length in enumerate(STORES):
        part = pl.ds(sum(STORES[:i]), length)
        parts.append(part)
        stores.append(pltpu.make_async_copy(result.at[:, part], out.at[:, part], out_sem.at[i]))
    for copy in fetches:
        copy.start()
    weights = transform_of(own[...] + other[...] + mine[...] + theirs[...])
    high = weights.astype(jnp.bfloat16)
    low = (weights - high.astype(jnp.float32)).astype(jnp.bfloat16)
    left = jnp.concatenate([high, low], axis=1)
    for copy in fetches:
        copy.wait()
    for part, copy in zip(parts, stores):
        block = held[:, part]
        both = jnp.concatenate([block, block], axis=0)
        result[:, part] = jnp.dot(left, both, preferred_element_type=jnp.float32).astype(
            jnp.bfloat16
        )
        copy.start()
    for copy in stores:
        copy.wait()


def analysis(own, other, mine, theirs, ensemble):
    members, width = ensemble.shape
    assert sum(STORES) == width
    return pl.pallas_call(
        analysis_kernel,
        in_specs=[pl.BlockSpec(memory_space=pltpu.VMEM)] * 4 + [pl.BlockSpec(memory_space=pltpu.HBM)],
        out_specs=pl.BlockSpec(memory_space=pltpu.HBM),
        out_shape=jax.ShapeDtypeStruct((members, width), jnp.bfloat16),
        scratch_shapes=[
            pltpu.VMEM((members, width), jnp.bfloat16),
            pltpu.VMEM((members, width), jnp.bfloat16),
            pltpu.SemaphoreType.DMA((FETCHES,)),
            pltpu.SemaphoreType.DMA((len(STORES),)),
        ],
        compiler_params=pltpu.CompilerParams(vmem_limit_bytes=VMEM_BYTES),
        name="analysis",
    )(own, other, mine, theirs, in_hbm(ensemble))


def local(n_tile, n_lev, ensemble, obs_pert, innovation, obs_rinv, loc_weight, obs_count):
    members = obs_pert.shape[0]
    axes = ("tile", "lev")

    def pairs(partner):
        return [
            (t * n_lev + l, (lambda a, b: a * n_lev + b)(*partner(t, l)))
            for t in range(n_tile)
            for l in range(n_lev)
        ]

    core = pairs(lambda t, l: (t, l ^ 1))
    high = pairs(lambda t, l: (t, l ^ 2))
    near = pairs(lambda t, l: (t ^ 1, l ^ (2 * (l & 1))))
    far = pairs(lambda t, l: ((t + 1 if t & 1 else t - 1) % n_tile, l ^ (2 * (l & 1))))

    parity = lax.rem(lax.axis_index("tile"), 2).astype(jnp.int32)
    gram = grams(
        obs_pert, innovation[None, :], obs_rinv[None, :], loc_weight, obs_count, parity[None]
    )
    gram = gram + lax.ppermute(gram, axes, core)
    to_far, to_near, own = gram[:members], gram[members : 2 * members], gram[2 * members :]
    from_far = lax.ppermute(to_far, axes, far)
    from_near = lax.ppermute(to_near, axes, near)
    other = lax.ppermute(own, axes, high)
    mine = from_far + from_near
    theirs = lax.ppermute(mine, axes, core)
    return analysis(own, other, mine, theirs, ensemble)


def solution(mesh):
    return jax.shard_map(
        functools.partial(local, mesh.shape["tile"], mesh.shape["lev"]),
        mesh=mesh,
        in_specs=(
            P(None, ("tile", "lev")),
            P(None, ("tile", "lev")),
            P(("tile", "lev")),
            P(("tile", "lev")),
            P(None, ("tile", "lev")),
            P(("tile", "lev")),
        ),
        out_specs=P(None, ("tile", "lev")),
        check_vma=False,
    )
```

```python
import functools
import math

import jax
import jax.numpy as jnp
from jax import lax
from jax.experimental import pallas as pl
from jax.experimental.pallas import tpu as pltpu
from jax.sharding import PartitionSpec as P

NS_STEPS = 10
OBS_CHUNKS = 2
SIDE_ROWS = 16
FETCHES = 4
STORES = (2048, 2048, 4096, 8192, 8192, 4096, 2048, 2048)
VMEM_BYTES = 40 * 1024 * 1024


def in_hbm(array):
    return pltpu.with_memory_space_constraint(array, pltpu.HBM)


def weighted_grams(rows, right):
    members = right.shape[0] - SIDE_ROWS
    left = jnp.concatenate([right[:members] * row for row in rows], axis=0)
    return lax.dot_general(left, right, (((1,), (1,)), ((), ())), preferred_element_type=jnp.float32)


def widened(gram):
    return jnp.concatenate(
        [gram, jnp.zeros((gram.shape[0], 128 - gram.shape[1]), jnp.float32)], axis=1
    )


def outer_kernel(
    count, place, pert, innov, rinv, loc, out, right, own, innov_in, rinv_in, loc_in, pert_sem, sem
):
    members, width = pert.shape
    chunk = width // OBS_CHUNKS
    sides = [
        pltpu.make_async_copy(source, target, sem.at[i])
        for i, (source, target) in enumerate(((rinv, rinv_in), (loc, loc_in), (innov, innov_in)))
    ]
    blocks = []
    for i in range(OBS_CHUNKS):
        part = pl.ds(i * chunk, chunk)
        target = right.at[pl.ds(0, members), part]
        blocks.append(pltpu.make_async_copy(pert.at[:, part], target, pert_sem.at[i]))
    for copy in sides + blocks:
        copy.start()
    for copy in sides:
        copy.wait()
    even = place[0] == 0
    total = None
    for i in range(OBS_CHUNKS):
        part = pl.ds(i * chunk, chunk)
        slots = i * chunk + lax.broadcasted_iota(jnp.int32, (1, chunk), 1)
        live = (slots < count[0]).astype(jnp.float32)
        scaled = rinv_in[:, part]
        before, mid, after = [
            (scaled * loc_in[j : j + 1, part] * live).astype(jnp.bfloat16) for j in range(3)
        ]
        own[:, part] = mid
        right[members:, part] = jnp.broadcast_to(
            innov_in[:, part].astype(jnp.bfloat16), (SIDE_ROWS, chunk)
        )
        rows = (jnp.where(even, before, after), jnp.where(even, after, before))
        blocks[i].wait()
        gram = weighted_grams(rows, right[:, part])
        total = gram if total is None else total + gram
    out[...] = widened(total)


def outer_grams(pert, innov, rinv, loc, count, place):
    members, width = pert.shape
    return pl.pallas_call(
        outer_kernel,
        in_specs=[pl.BlockSpec(memory_space=pltpu.SMEM)] * 2
        + [pl.BlockSpec(memory_space=pltpu.HBM)] * 4,
        out_specs=[pl.BlockSpec(memory_space=pltpu.VMEM)] * 3,
        out_shape=[
            jax.ShapeDtypeStruct((2 * members, 128), jnp.float32),
            jax.ShapeDtypeStruct((members + SIDE_ROWS, width), jnp.bfloat16),
            jax.ShapeDtypeStruct((1, width), jnp.bfloat16),
        ],
        scratch_shapes=[
            pltpu.VMEM((1, width), jnp.float32),
            pltpu.VMEM((1, width), jnp.float32),
            pltpu.VMEM((3, width), jnp.float32),
            pltpu.SemaphoreType.DMA((OBS_CHUNKS,)),
            pltpu.SemaphoreType.DMA((3,)),
        ],
        compiler_params=pltpu.CompilerParams(vmem_limit_bytes=VMEM_BYTES),
        name="outer_grams",
    )(count, place, *(in_hbm(x) for x in (pert, innov, rinv, loc)))


def own_kernel(right, own, out):
    out[...] = widened(weighted_grams((own[...],), right[...]))


def own_gram(right, own):
    members = right.shape[0] - SIDE_ROWS
    width = right.shape[1]
    return pl.pallas_call(
        own_kernel,
        in_specs=[pl.BlockSpec(memory_space=pltpu.VMEM)] * 2,
        out_specs=pl.BlockSpec(memory_space=pltpu.VMEM),
        out_shape=jax.ShapeDtypeStruct((members, 128), jnp.float32),
        compiler_params=pltpu.CompilerParams(vmem_limit_bytes=VMEM_BYTES),
        cost_estimate=pl.CostEstimate(
            flops=2 * members * 128 * width, bytes_accessed=2 * right.size, transcendentals=0
        ),
        name="own_gram",
    )(right, own)


def split(array):
    high = array.astype(jnp.bfloat16)
    rest = array - high.astype(jnp.float32)
    middle = rest.astype(jnp.bfloat16)
    return high, middle, (rest - middle.astype(jnp.float32)).astype(jnp.bfloat16)


def dot(a, b):
    return jnp.dot(a, b, preferred_element_type=jnp.float32)


def product(a, b):
    high, middle, low = a
    below = jnp.zeros((128 - b[0].shape[0], 128), jnp.bfloat16)
    b_high, b_middle, b_low = (jnp.concatenate([part, below], axis=0) for part in b)
    pair = jnp.concatenate([b_high, b_middle], axis=1)
    large = dot(jnp.concatenate([high, middle], axis=1), jnp.concatenate([pair, pair], axis=0))
    small = dot(jnp.concatenate([low, high], axis=1), jnp.concatenate([b_high, b_low], axis=0))
    return (small + large[:, 128:]) + large[:, :128]


def transform_of(total):
    members = total.shape[0]
    rows = lax.broadcasted_iota(jnp.int32, total.shape, 0)
    cols = lax.broadcasted_iota(jnp.int32, total.shape, 1)
    eye = (rows == cols).astype(jnp.float32)
    square = cols < members
    wide = jnp.where(cols <= members, total, 0.0) + (members - 1.0) * eye
    mat = jnp.where(square, wide, 0.0)
    proj = wide - mat
    parts = split(wide)
    squared = product(parts, parts)
    inv = 1.0 / jnp.sqrt(jnp.sum(mat * mat, keepdims=True))
    head = jnp.where(square, squared, 0.0)
    iterate = split((1.5 * inv) * mat - (0.5 * inv * inv) * head)
    inverse_root = 1.5 * (eye + proj) - (0.5 * inv) * (mat + (squared - head))
    for step in range(1, NS_STEPS):
        root_parts = split(inverse_root)
        factor = split(1.5 * eye - 0.5 * product(root_parts, iterate))
        if step < NS_STEPS - 1:
            iterate = split(product(iterate, factor))
        inverse_root = product(factor, root_parts)
    root = jnp.where(square, inverse_root, 0.0)
    mean_weight = inv * jnp.sum(
        root * inverse_root[:, members : members + 1], axis=0, keepdims=True
    )
    scaled = root * (math.sqrt(members - 1.0) * jnp.sqrt(inv))
    transform = (scaled + mean_weight).astype(jnp.bfloat16).astype(jnp.float32)[:, :members]
    keep = 1.0 - jnp.sum(transform, axis=1, keepdims=True)
    return transform + keep / members


def analysis_kernel(own, high, mine, theirs, ensemble, out, held, result, in_sem, out_sem):
    members, width = held.shape
    chunk = width // FETCHES
    fetches, stores, parts = [], [], []
    for i in range(FETCHES):
        part = pl.ds(i * chunk, chunk)
        fetches.append(pltpu.make_async_copy(ensemble.at[:, part], held.at[:, part], in_sem.at[i]))
    for i, length in enumerate(STORES):
        part = pl.ds(sum(STORES[:i]), length)
        parts.append(part)
        stores.append(pltpu.make_async_copy(result.at[:, part], out.at[:, part], out_sem.at[i]))
    for copy in fetches:
        copy.start()
    weights = transform_of((own[...] + high[...]) + (mine[...] + theirs[...]))
    high = weights.astype(jnp.bfloat16)
    low = (weights - high.astype(jnp.float32)).astype(jnp.bfloat16)
    left = jnp.concatenate([high, low], axis=1)
    for copy in fetches:
        copy.wait()
    for part, copy in zip(parts, stores):
        block = held[:, part]
        both = jnp.concatenate([block, block], axis=0)
        result[:, part] = jnp.dot(left, both, preferred_element_type=jnp.float32).astype(
            jnp.bfloat16
        )
        copy.start()
    for copy in stores:
        copy.wait()


def analysis(grams, ensemble):
    members, width = ensemble.shape
    assert sum(STORES) == width
    return pl.pallas_call(
        analysis_kernel,
        in_specs=[pl.BlockSpec(memory_space=pltpu.VMEM)] * len(grams) + [pl.BlockSpec(memory_space=pltpu.HBM)],
        out_specs=pl.BlockSpec(memory_space=pltpu.HBM),
        out_shape=jax.ShapeDtypeStruct((members, width), jnp.bfloat16),
        scratch_shapes=[
            pltpu.VMEM((members, width), jnp.bfloat16),
            pltpu.VMEM((members, width), jnp.bfloat16),
            pltpu.SemaphoreType.DMA((FETCHES,)),
            pltpu.SemaphoreType.DMA((len(STORES),)),
        ],
        compiler_params=pltpu.CompilerParams(vmem_limit_bytes=VMEM_BYTES),
        name="analysis",
    )(*grams, in_hbm(ensemble))


def local(n_tile, n_lev, ensemble, obs_pert, innovation, obs_rinv, loc_weight, obs_count):
    members = obs_pert.shape[0]
    axes = ("tile", "lev")

    def pairs(partner):
        return [
            (t * n_lev + l, (lambda a, b: a * n_lev + b)(*partner(t, l)))
            for t in range(n_tile)
            for l in range(n_lev)
        ]

    core = pairs(lambda t, l: (t, l ^ 1))
    high = pairs(lambda t, l: (t, l ^ 2))
    near = pairs(lambda t, l: (t ^ 1, l ^ (2 * (l & 1))))
    far = pairs(lambda t, l: ((t + 1 if t & 1 else t - 1) % n_tile, l ^ (2 * (l & 1))))
    place = (lax.axis_index("tile") % 2).astype(jnp.int32)
    outer, right, weight = outer_grams(
        obs_pert, innovation[None, :], obs_rinv[None, :], loc_weight, obs_count, place[None]
    )
    own = own_gram(right, weight)
    members = own.shape[0]
    outer = outer + lax.ppermute(outer, axes, core)
    own = own + lax.ppermute(own, axes, core)
    from_far = lax.ppermute(outer[:members], axes, far)
    from_near = lax.ppermute(outer[members:], axes, near)
    mine = from_far + from_near
    from_high = lax.ppermute(own, axes, high)
    return analysis((own, from_high, mine, lax.ppermute(mine, axes, core)), ensemble)


def solution(mesh):
    return jax.shard_map(
        functools.partial(local, mesh.shape["tile"], mesh.shape["lev"]),
        mesh=mesh,
        in_specs=(
            P(None, ("tile", "lev")),
            P(None, ("tile", "lev")),
            P(("tile", "lev")),
            P(("tile", "lev")),
            P(None, ("tile", "lev")),
            P(("tile", "lev")),
        ),
        out_specs=P(None, ("tile", "lev")),
        check_vma=False,
    )
```

```python
import functools
import math

import jax
import jax.numpy as jnp
from jax import lax
from jax.experimental import pallas as pl
from jax.experimental.pallas import tpu as pltpu
from jax.sharding import PartitionSpec as P

NS_STEPS = 10
OBS_CHUNKS = (16384,)
SIDE_ROWS = 16
FETCHES = 4
STORES = 16
VMEM_BYTES = 40 * 1024 * 1024


def in_hbm(array):
    return pltpu.with_memory_space_constraint(array, pltpu.HBM)


def weighted_grams(rows, right):
    members = right.shape[0] - SIDE_ROWS
    left = jnp.concatenate([right[:members] * row for row in rows], axis=0)
    return lax.dot_general(left, right, (((1,), (1,)), ((), ())), preferred_element_type=jnp.float32)


def widened(gram):
    return jnp.concatenate(
        [gram, jnp.zeros((gram.shape[0], 128 - gram.shape[1]), jnp.float32)], axis=1
    )


def outer_kernel(
    count, pert, innov, rinv, loc, before_out, after_out, right, own, innov_in, rinv_in, loc_in, pert_sem, sem
):
    members, width = pert.shape
    assert sum(OBS_CHUNKS) == width
    parts = [(sum(OBS_CHUNKS[:i]), length) for i, length in enumerate(OBS_CHUNKS)]
    sides = [
        pltpu.make_async_copy(source, target, sem.at[i])
        for i, (source, target) in enumerate(((rinv, rinv_in), (loc, loc_in), (innov, innov_in)))
    ]
    blocks = []
    for i, (start, length) in enumerate(parts):
        part = pl.ds(start, length)
        target = right.at[pl.ds(0, members), part]
        blocks.append(pltpu.make_async_copy(pert.at[:, part], target, pert_sem.at[i]))
    for copy in sides + blocks:
        copy.start()
    for copy in sides:
        copy.wait()
    total = None
    for copy, (start, length) in zip(blocks, parts):
        part = pl.ds(start, length)
        slots = start + lax.broadcasted_iota(jnp.int32, (1, length), 1)
        live = (slots < count[0]).astype(jnp.float32)
        scaled = rinv_in[:, part]
        before, mid, after = [
            (scaled * loc_in[j : j + 1, part] * live).astype(jnp.bfloat16) for j in range(3)
        ]
        own[:, part] = mid
        right[members:, part] = jnp.broadcast_to(
            innov_in[:, part].astype(jnp.bfloat16), (SIDE_ROWS, length)
        )
        rows = (before, after)
        copy.wait()
        gram = weighted_grams(rows, right[:, part])
        total = gram if total is None else total + gram
    before_out[...] = widened(total[:members])
    after_out[...] = widened(total[members:])


def outer_grams(pert, innov, rinv, loc, count):
    members, width = pert.shape
    return pl.pallas_call(
        outer_kernel,
        in_specs=[pl.BlockSpec(memory_space=pltpu.SMEM)]
        + [pl.BlockSpec(memory_space=pltpu.HBM)] * 4,
        out_specs=[pl.BlockSpec(memory_space=pltpu.VMEM)] * 4,
        out_shape=[
            jax.ShapeDtypeStruct((members, 128), jnp.float32),
            jax.ShapeDtypeStruct((members, 128), jnp.float32),
            jax.ShapeDtypeStruct((members + SIDE_ROWS, width), jnp.bfloat16),
            jax.ShapeDtypeStruct((1, width), jnp.bfloat16),
        ],
        scratch_shapes=[
            pltpu.VMEM((1, width), jnp.float32),
            pltpu.VMEM((1, width), jnp.float32),
            pltpu.VMEM((3, width), jnp.float32),
            pltpu.SemaphoreType.DMA((len(OBS_CHUNKS),)),
            pltpu.SemaphoreType.DMA((3,)),
        ],
        compiler_params=pltpu.CompilerParams(vmem_limit_bytes=VMEM_BYTES),
        name="outer_grams",
    )(count, *(in_hbm(x) for x in (pert, innov, rinv, loc)))


def own_kernel(right, own, out):
    out[...] = widened(weighted_grams((own[...],), right[...]))


def own_gram(right, own):
    members = right.shape[0] - SIDE_ROWS
    width = right.shape[1]
    return pl.pallas_call(
        own_kernel,
        in_specs=[pl.BlockSpec(memory_space=pltpu.VMEM)] * 2,
        out_specs=pl.BlockSpec(memory_space=pltpu.VMEM),
        out_shape=jax.ShapeDtypeStruct((members, 128), jnp.float32),
        compiler_params=pltpu.CompilerParams(vmem_limit_bytes=VMEM_BYTES),
        cost_estimate=pl.CostEstimate(
            flops=2 * members * 128 * width, bytes_accessed=2 * right.size, transcendentals=0
        ),
        name="own_gram",
    )(right, own)


def split(array):
    high = array.astype(jnp.bfloat16)
    rest = array - high.astype(jnp.float32)
    middle = rest.astype(jnp.bfloat16)
    return high, middle, (rest - middle.astype(jnp.float32)).astype(jnp.bfloat16)


def dot(a, b):
    return jnp.dot(a, b, preferred_element_type=jnp.float32)


def product(a, b):
    high, middle, low = a
    below = jnp.zeros((128 - b[0].shape[0], 128), jnp.bfloat16)
    b_high, b_middle, b_low = (jnp.concatenate([part, below], axis=0) for part in b)
    pair = jnp.concatenate([b_high, b_middle], axis=1)
    large = dot(jnp.concatenate([high, middle], axis=1), jnp.concatenate([pair, pair], axis=0))
    small = dot(jnp.concatenate([low, high], axis=1), jnp.concatenate([b_high, b_low], axis=0))
    return (small + large[:, 128:]) + large[:, :128]


def transform_of(total):
    members = total.shape[0]
    rows = lax.broadcasted_iota(jnp.int32, total.shape, 0)
    cols = lax.broadcasted_iota(jnp.int32, total.shape, 1)
    eye = (rows == cols).astype(jnp.float32)
    square = cols < members
    wide = jnp.where(cols <= members, total, 0.0) + (members - 1.0) * eye
    mat = jnp.where(square, wide, 0.0)
    proj = wide - mat
    parts = split(wide)
    squared = product(parts, parts)
    inv = 1.0 / jnp.sqrt(jnp.sum(mat * mat, keepdims=True))
    head = jnp.where(square, squared, 0.0)
    iterate = split((1.5 * inv) * mat - (0.5 * inv * inv) * head)
    inverse_root = 1.5 * (eye + proj) - (0.5 * inv) * (mat + (squared - head))
    for step in range(1, NS_STEPS):
        root_parts = split(inverse_root)
        factor = split(1.5 * eye - 0.5 * product(root_parts, iterate))
        if step < NS_STEPS - 1:
            iterate = split(product(iterate, factor))
        inverse_root = product(factor, root_parts)
    root = jnp.where(square, inverse_root, 0.0)
    mean_weight = inv * jnp.sum(
        root * inverse_root[:, members : members + 1], axis=0, keepdims=True
    )
    scaled = root * (math.sqrt(members - 1.0) * jnp.sqrt(inv))
    return (scaled + mean_weight).astype(jnp.bfloat16)[:, :members]


def analysis_kernel(mine, theirs, ensemble, out, held, result, in_sem, out_sem):
    members, width = held.shape
    fetches, stores, parts = [], [], []
    for i in range(FETCHES):
        part = pl.ds(i * (width // FETCHES), width // FETCHES)
        fetches.append(pltpu.make_async_copy(ensemble.at[:, part], held.at[:, part], in_sem.at[i]))
    for i in range(STORES):
        part = pl.ds(i * (width // STORES), width // STORES)
        parts.append(part)
        stores.append(pltpu.make_async_copy(result.at[:, part], out.at[:, part], out_sem.at[i]))
    for copy in fetches:
        copy.start()
    transform = transform_of(mine[...] + theirs[...])
    share = (1.0 - jnp.sum(transform.astype(jnp.float32), axis=1, keepdims=True)) / members
    left = jnp.concatenate([transform, jnp.ones((SIDE_ROWS, members), jnp.bfloat16)], axis=0)
    for copy in fetches:
        copy.wait()
    for part, copy in zip(parts, stores):
        sums = dot(left, held[:, part])
        mean = share * sums[members : members + 1]
        result[:, part] = (sums[:members] + mean).astype(jnp.bfloat16)
        copy.start()
    for copy in stores:
        copy.wait()


def analysis(grams, ensemble):
    members, width = ensemble.shape
    return pl.pallas_call(
        analysis_kernel,
        in_specs=[pl.BlockSpec(memory_space=pltpu.VMEM)] * len(grams) + [pl.BlockSpec(memory_space=pltpu.HBM)],
        out_specs=pl.BlockSpec(memory_space=pltpu.HBM),
        out_shape=jax.ShapeDtypeStruct((members, width), jnp.bfloat16),
        scratch_shapes=[
            pltpu.VMEM((members, width), jnp.bfloat16),
            pltpu.VMEM((members, width), jnp.bfloat16),
            pltpu.SemaphoreType.DMA((FETCHES,)),
            pltpu.SemaphoreType.DMA((STORES,)),
        ],
        compiler_params=pltpu.CompilerParams(vmem_limit_bytes=VMEM_BYTES),
        name="analysis",
    )(*grams, in_hbm(ensemble))


def local(n_tile, n_lev, ensemble, obs_pert, innovation, obs_rinv, loc_weight, obs_count):
    members = obs_pert.shape[0]
    axes = ("tile", "lev")

    def pairs(partner):
        return [
            (t * n_lev + l, (lambda a, b: a * n_lev + b)(*partner(t, l)))
            for t in range(n_tile)
            for l in range(n_lev)
        ]

    core = pairs(lambda t, l: (t, l ^ 1))
    high = pairs(lambda t, l: (t, l ^ 2))
    onward = pairs(lambda t, l: ((t + 1) % n_tile, l ^ (2 * (l & 1))))
    back = pairs(lambda t, l: ((t - 1) % n_tile, l ^ (2 * (l & 1))))
    before, after, right, weight = outer_grams(
        obs_pert, innovation[None, :], obs_rinv[None, :], loc_weight, obs_count
    )
    own = own_gram(right, weight)
    after = after + lax.ppermute(after, axes, core)
    before = before + lax.ppermute(before, axes, core)
    after, own = lax.optimization_barrier((after, own))
    from_before = lax.ppermute(after, axes, onward)
    from_after = lax.ppermute(before, axes, back)
    from_high = lax.ppermute(own, axes, high)
    mine = (own + from_high) + from_after + from_before
    return analysis((mine, lax.ppermute(mine, axes, core)), ensemble)


def solution(mesh):
    return jax.shard_map(
        functools.partial(local, mesh.shape["tile"], mesh.shape["lev"]),
        mesh=mesh,
        in_specs=(
            P(None, ("tile", "lev")),
            P(None, ("tile", "lev")),
            P(("tile", "lev")),
            P(("tile", "lev")),
            P(None, ("tile", "lev")),
            P(("tile", "lev")),
        ),
        out_specs=P(None, ("tile", "lev")),
        check_vma=False,
    )
```

```python
import functools
import math

import jax
import jax.numpy as jnp
from jax import lax
from jax.experimental import pallas as pl
from jax.experimental.pallas import tpu as pltpu
from jax.sharding import PartitionSpec as P

NS_STEPS = 10
OBS_CHUNKS = (16384,)
SIDE_ROWS = 16
FETCHES = 4
STORES = 16
VMEM_BYTES = 40 * 1024 * 1024


def in_hbm(array):
    return pltpu.with_memory_space_constraint(array, pltpu.HBM)


def weighted_grams(rows, right):
    members = right.shape[0] - SIDE_ROWS
    left = jnp.concatenate([right[:members] * row for row in rows], axis=0)
    return lax.dot_general(left, right, (((1,), (1,)), ((), ())), preferred_element_type=jnp.float32)


def widened(gram):
    return jnp.concatenate(
        [gram, jnp.zeros((gram.shape[0], 128 - gram.shape[1]), jnp.float32)], axis=1
    )


def outer_kernel(
    count, pert, innov, rinv, loc, out, right, own, innov_in, rinv_in, loc_in, pert_sem, sem
):
    members, width = pert.shape
    assert sum(OBS_CHUNKS) == width
    parts = [(sum(OBS_CHUNKS[:i]), length) for i, length in enumerate(OBS_CHUNKS)]
    sides = [
        pltpu.make_async_copy(source, target, sem.at[i])
        for i, (source, target) in enumerate(((rinv, rinv_in), (loc, loc_in), (innov, innov_in)))
    ]
    blocks = []
    for i, (start, length) in enumerate(parts):
        part = pl.ds(start, length)
        target = right.at[pl.ds(0, members), part]
        blocks.append(pltpu.make_async_copy(pert.at[:, part], target, pert_sem.at[i]))
    for copy in sides + blocks:
        copy.start()
    for copy in sides:
        copy.wait()
    total = None
    for copy, (start, length) in zip(blocks, parts):
        part = pl.ds(start, length)
        slots = start + lax.broadcasted_iota(jnp.int32, (1, length), 1)
        live = (slots < count[0]).astype(jnp.float32)
        scaled = rinv_in[:, part]
        before, mid, after = [
            (scaled * loc_in[j : j + 1, part] * live).astype(jnp.bfloat16) for j in range(3)
        ]
        own[:, part] = mid
        right[members:, part] = jnp.broadcast_to(
            innov_in[:, part].astype(jnp.bfloat16), (SIDE_ROWS, length)
        )
        rows = (before, after)
        copy.wait()
        gram = weighted_grams(rows, right[:, part])
        total = gram if total is None else total + gram
    out[...] = widened(total)


def outer_grams(pert, innov, rinv, loc, count):
    members, width = pert.shape
    return pl.pallas_call(
        outer_kernel,
        in_specs=[pl.BlockSpec(memory_space=pltpu.SMEM)]
        + [pl.BlockSpec(memory_space=pltpu.HBM)] * 4,
        out_specs=[pl.BlockSpec(memory_space=pltpu.VMEM)] * 3,
        out_shape=[
            jax.ShapeDtypeStruct((2 * members, 128), jnp.float32),
            jax.ShapeDtypeStruct((members + SIDE_ROWS, width), jnp.bfloat16),
            jax.ShapeDtypeStruct((1, width), jnp.bfloat16),
        ],
        scratch_shapes=[
            pltpu.VMEM((1, width), jnp.float32),
            pltpu.VMEM((1, width), jnp.float32),
            pltpu.VMEM((3, width), jnp.float32),
            pltpu.SemaphoreType.DMA((len(OBS_CHUNKS),)),
            pltpu.SemaphoreType.DMA((3,)),
        ],
        compiler_params=pltpu.CompilerParams(vmem_limit_bytes=VMEM_BYTES),
        name="outer_grams",
    )(count, *(in_hbm(x) for x in (pert, innov, rinv, loc)))


def own_kernel(right, own, out):
    out[...] = widened(weighted_grams((own[...],), right[...]))


def own_gram(right, own):
    members = right.shape[0] - SIDE_ROWS
    width = right.shape[1]
    return pl.pallas_call(
        own_kernel,
        in_specs=[pl.BlockSpec(memory_space=pltpu.VMEM)] * 2,
        out_specs=pl.BlockSpec(memory_space=pltpu.VMEM),
        out_shape=jax.ShapeDtypeStruct((members, 128), jnp.float32),
        compiler_params=pltpu.CompilerParams(vmem_limit_bytes=VMEM_BYTES),
        cost_estimate=pl.CostEstimate(
            flops=2 * members * 128 * width, bytes_accessed=2 * right.size, transcendentals=0
        ),
        name="own_gram",
    )(right, own)


def split(array):
    high = array.astype(jnp.bfloat16)
    rest = array - high.astype(jnp.float32)
    middle = rest.astype(jnp.bfloat16)
    return high, middle, (rest - middle.astype(jnp.float32)).astype(jnp.bfloat16)


def dot(a, b):
    return jnp.dot(a, b, preferred_element_type=jnp.float32)


def product(a, b):
    high, middle, low = a
    below = jnp.zeros((128 - b[0].shape[0], 128), jnp.bfloat16)
    b_high, b_middle, b_low = (jnp.concatenate([part, below], axis=0) for part in b)
    pair = jnp.concatenate([b_high, b_middle], axis=1)
    large = dot(jnp.concatenate([high, middle], axis=1), jnp.concatenate([pair, pair], axis=0))
    small = dot(jnp.concatenate([low, high], axis=1), jnp.concatenate([b_high, b_low], axis=0))
    return (small + large[:, 128:]) + large[:, :128]


def transform_of(total):
    members = total.shape[0]
    rows = lax.broadcasted_iota(jnp.int32, total.shape, 0)
    cols = lax.broadcasted_iota(jnp.int32, total.shape, 1)
    eye = (rows == cols).astype(jnp.float32)
    square = cols < members
    mat = jnp.where(square, total, 0.0) + (members - 1.0) * eye
    proj = jnp.where(cols == members, total, 0.0)
    mat_parts = split(mat)
    squared = product(mat_parts, mat_parts)
    inv = 1.0 / jnp.sqrt(jnp.sum(mat * mat, keepdims=True))
    first = mat * inv
    second = squared * (inv * inv)
    inverse_root = eye + proj
    for triple in range((NS_STEPS - 1) // 3):
        first_parts = split(first)
        if triple:
            second = product(first_parts, first_parts)
        second_parts = split(second)
        third = product(second_parts, first_parts)
        fourth = product(second_parts, second_parts)
        pair = 2.25 * eye - 2.4375 * first + 1.6875 * second - 0.5625 * third + 0.0625 * fourth
        pair_parts = split(pair)
        pair_squared = split(product(pair_parts, pair_parts))
        first_pair = product(first_parts, pair_parts)
        second_pair = split(product(second_parts, pair_parts))
        factor = split(1.5 * pair - 0.5 * product(pair_squared, split(first_pair)))
        scaled = split(1.5 * first_pair - 0.5 * product(second_pair, pair_squared))
        first = product(scaled, factor)
        inverse_root = product(factor, split(inverse_root))
    inverse_root = product(split(1.5 * eye - 0.5 * first), split(inverse_root))
    root = jnp.where(square, inverse_root, 0.0)
    mean_weight = inv * jnp.sum(
        root * inverse_root[:, members : members + 1], axis=0, keepdims=True
    )
    scaled = root * (math.sqrt(members - 1.0) * jnp.sqrt(inv))
    return (scaled + mean_weight).astype(jnp.bfloat16)[:, :members]


def analysis_kernel(mine, theirs, ensemble, out, held, result, in_sem, out_sem):
    members, width = held.shape
    fetches, stores, parts = [], [], []
    for i in range(FETCHES):
        part = pl.ds(i * (width // FETCHES), width // FETCHES)
        fetches.append(pltpu.make_async_copy(ensemble.at[:, part], held.at[:, part], in_sem.at[i]))
    for i in range(STORES):
        part = pl.ds(i * (width // STORES), width // STORES)
        parts.append(part)
        stores.append(pltpu.make_async_copy(result.at[:, part], out.at[:, part], out_sem.at[i]))
    for copy in fetches:
        copy.start()
    transform = transform_of(mine[...] + theirs[...])
    share = (1.0 - jnp.sum(transform.astype(jnp.float32), axis=1, keepdims=True)) / members
    left = jnp.concatenate([transform, jnp.ones((SIDE_ROWS, members), jnp.bfloat16)], axis=0)
    for copy in fetches:
        copy.wait()
    for part, copy in zip(parts, stores):
        sums = dot(left, held[:, part])
        mean = share * sums[members : members + 1]
        result[:, part] = (sums[:members] + mean).astype(jnp.bfloat16)
        copy.start()
    for copy in stores:
        copy.wait()


def analysis(grams, ensemble):
    members, width = ensemble.shape
    return pl.pallas_call(
        analysis_kernel,
        in_specs=[pl.BlockSpec(memory_space=pltpu.VMEM)] * len(grams) + [pl.BlockSpec(memory_space=pltpu.HBM)],
        out_specs=pl.BlockSpec(memory_space=pltpu.HBM),
        out_shape=jax.ShapeDtypeStruct((members, width), jnp.bfloat16),
        scratch_shapes=[
            pltpu.VMEM((members, width), jnp.bfloat16),
            pltpu.VMEM((members, width), jnp.bfloat16),
            pltpu.SemaphoreType.DMA((FETCHES,)),
            pltpu.SemaphoreType.DMA((STORES,)),
        ],
        compiler_params=pltpu.CompilerParams(vmem_limit_bytes=VMEM_BYTES),
        name="analysis",
    )(*grams, in_hbm(ensemble))


def local(n_tile, n_lev, ensemble, obs_pert, innovation, obs_rinv, loc_weight, obs_count):
    members = obs_pert.shape[0]
    axes = ("tile", "lev")

    def pairs(partner):
        return [
            (t * n_lev + l, (lambda a, b: a * n_lev + b)(*partner(t, l)))
            for t in range(n_tile)
            for l in range(n_lev)
        ]

    core = pairs(lambda t, l: (t, l ^ 1))
    high = pairs(lambda t, l: (t, l ^ 2))
    onward = pairs(lambda t, l: ((t + 1) % n_tile, l ^ (2 * (l & 1))))
    back = pairs(lambda t, l: ((t - 1) % n_tile, l ^ (2 * (l & 1))))
    outer, right, weight = outer_grams(
        obs_pert, innovation[None, :], obs_rinv[None, :], loc_weight, obs_count
    )
    own = own_gram(right, weight)
    members = own.shape[0]
    outer = outer + lax.ppermute(outer, axes, core)
    before, after = outer[:members], outer[members:]
    after, own = lax.optimization_barrier((after, own))
    from_before = lax.ppermute(after, axes, onward)
    from_after = lax.ppermute(before, axes, back)
    from_high = lax.ppermute(own, axes, high)
    mine = from_after + (own + from_high) + from_before
    return analysis((mine, lax.ppermute(mine, axes, core)), ensemble)


def solution(mesh):
    return jax.shard_map(
        functools.partial(local, mesh.shape["tile"], mesh.shape["lev"]),
        mesh=mesh,
        in_specs=(
            P(None, ("tile", "lev")),
            P(None, ("tile", "lev")),
            P(("tile", "lev")),
            P(("tile", "lev")),
            P(None, ("tile", "lev")),
            P(("tile", "lev")),
        ),
        out_specs=P(None, ("tile", "lev")),
        check_vma=False,
    )
```

```python
import functools
import math

import jax
import jax.numpy as jnp
from jax import lax
from jax.experimental import pallas as pl
from jax.experimental.pallas import tpu as pltpu
from jax.sharding import PartitionSpec as P

NS_STEPS = 10
OBS_CHUNKS = (16384,)
SIDE_ROWS = 16
FETCHES = 4
STORES = 16
VMEM_BYTES = 40 * 1024 * 1024


def in_hbm(array):
    return pltpu.with_memory_space_constraint(array, pltpu.HBM)


def weighted_grams(rows, right):
    members = right.shape[0] - SIDE_ROWS
    left = jnp.concatenate([right[:members] * row for row in rows], axis=0)
    return lax.dot_general(left, right, (((1,), (1,)), ((), ())), preferred_element_type=jnp.float32)


def widened(gram):
    return jnp.concatenate(
        [gram, jnp.zeros((gram.shape[0], 128 - gram.shape[1]), jnp.float32)], axis=1
    )


def next_kernel(
    count, pert, innov, rinv, loc, out, right, first, second, innov_in, rinv_in, loc_in, pert_sem, sem
):
    members, width = pert.shape
    assert sum(OBS_CHUNKS) == width
    parts = [(sum(OBS_CHUNKS[:i]), length) for i, length in enumerate(OBS_CHUNKS)]
    sides = [
        pltpu.make_async_copy(source, target, sem.at[i])
        for i, (source, target) in enumerate(((rinv, rinv_in), (loc, loc_in), (innov, innov_in)))
    ]
    blocks = []
    for i, (start, length) in enumerate(parts):
        part = pl.ds(start, length)
        target = right.at[pl.ds(0, members), part]
        blocks.append(pltpu.make_async_copy(pert.at[:, part], target, pert_sem.at[i]))
    for copy in sides + blocks:
        copy.start()
    for copy in sides:
        copy.wait()
    total = None
    for copy, (start, length) in zip(blocks, parts):
        part = pl.ds(start, length)
        slots = start + lax.broadcasted_iota(jnp.int32, (1, length), 1)
        live = (slots < count[0]).astype(jnp.float32)
        scaled = rinv_in[:, part]
        before, mid, after = [
            (scaled * loc_in[j : j + 1, part] * live).astype(jnp.bfloat16) for j in range(3)
        ]
        first[:, part] = before
        second[:, part] = mid
        right[members:, part] = jnp.broadcast_to(
            innov_in[:, part].astype(jnp.bfloat16), (SIDE_ROWS, length)
        )
        copy.wait()
        gram = weighted_grams((after,), right[:, part])
        total = gram if total is None else total + gram
    out[...] = widened(total)


def next_gram(pert, innov, rinv, loc, count):
    members, width = pert.shape
    return pl.pallas_call(
        next_kernel,
        in_specs=[pl.BlockSpec(memory_space=pltpu.SMEM)]
        + [pl.BlockSpec(memory_space=pltpu.HBM)] * 4,
        out_specs=[pl.BlockSpec(memory_space=pltpu.VMEM)] * 4,
        out_shape=[
            jax.ShapeDtypeStruct((members, 128), jnp.float32),
            jax.ShapeDtypeStruct((members + SIDE_ROWS, width), jnp.bfloat16),
            jax.ShapeDtypeStruct((1, width), jnp.bfloat16),
            jax.ShapeDtypeStruct((1, width), jnp.bfloat16),
        ],
        scratch_shapes=[
            pltpu.VMEM((1, width), jnp.float32),
            pltpu.VMEM((1, width), jnp.float32),
            pltpu.VMEM((3, width), jnp.float32),
            pltpu.SemaphoreType.DMA((len(OBS_CHUNKS),)),
            pltpu.SemaphoreType.DMA((3,)),
        ],
        compiler_params=pltpu.CompilerParams(vmem_limit_bytes=VMEM_BYTES),
        name="next_gram",
    )(count, *(in_hbm(x) for x in (pert, innov, rinv, loc)))


def one_kernel(right, own, out):
    out[...] = widened(weighted_grams((own[...],), right[...]))


def one_gram(right, own):
    members = right.shape[0] - SIDE_ROWS
    width = right.shape[1]
    return pl.pallas_call(
        one_kernel,
        in_specs=[pl.BlockSpec(memory_space=pltpu.VMEM)] * 2,
        out_specs=pl.BlockSpec(memory_space=pltpu.VMEM),
        out_shape=jax.ShapeDtypeStruct((members, 128), jnp.float32),
        compiler_params=pltpu.CompilerParams(vmem_limit_bytes=VMEM_BYTES),
        cost_estimate=pl.CostEstimate(
            flops=2 * members * 128 * width, bytes_accessed=2 * right.size, transcendentals=0
        ),
        name="one_gram",
    )(right, own)


def split(array):
    high = array.astype(jnp.bfloat16)
    rest = array - high.astype(jnp.float32)
    middle = rest.astype(jnp.bfloat16)
    return high, middle, (rest - middle.astype(jnp.float32)).astype(jnp.bfloat16)


def dot(a, b):
    return jnp.dot(a, b, preferred_element_type=jnp.float32)


def product(a, b):
    high, middle, low = a
    below = jnp.zeros((128 - b[0].shape[0], 128), jnp.bfloat16)
    b_high, b_middle, b_low = (jnp.concatenate([part, below], axis=0) for part in b)
    pair = jnp.concatenate([b_high, b_middle], axis=1)
    large = dot(jnp.concatenate([high, middle], axis=1), jnp.concatenate([pair, pair], axis=0))
    small = dot(jnp.concatenate([low, high], axis=1), jnp.concatenate([b_high, b_low], axis=0))
    return (small + large[:, 128:]) + large[:, :128]


def transform_of(total):
    members = total.shape[0]
    rows = lax.broadcasted_iota(jnp.int32, total.shape, 0)
    cols = lax.broadcasted_iota(jnp.int32, total.shape, 1)
    eye = (rows == cols).astype(jnp.float32)
    square = cols < members
    mat = jnp.where(square, total, 0.0) + (members - 1.0) * eye
    proj = jnp.where(cols == members, total, 0.0)
    mat_parts = split(mat)
    squared = product(mat_parts, mat_parts)
    inv = 1.0 / jnp.sqrt(jnp.sum(mat * mat, keepdims=True))
    first = mat * inv
    second = squared * (inv * inv)
    inverse_root = eye + proj
    for triple in range((NS_STEPS - 1) // 3):
        first_parts = split(first)
        if triple:
            second = product(first_parts, first_parts)
        second_parts = split(second)
        third = product(second_parts, first_parts)
        fourth = product(second_parts, second_parts)
        pair = 2.25 * eye - 2.4375 * first + 1.6875 * second - 0.5625 * third + 0.0625 * fourth
        pair_parts = split(pair)
        pair_squared = split(product(pair_parts, pair_parts))
        first_pair = product(first_parts, pair_parts)
        second_pair = split(product(second_parts, pair_parts))
        factor = split(1.5 * pair - 0.5 * product(pair_squared, split(first_pair)))
        scaled = split(1.5 * first_pair - 0.5 * product(second_pair, pair_squared))
        first = product(scaled, factor)
        inverse_root = product(factor, split(inverse_root))
    inverse_root = product(split(1.5 * eye - 0.5 * first), split(inverse_root))
    root = jnp.where(square, inverse_root, 0.0)
    mean_weight = inv * jnp.sum(
        root * inverse_root[:, members : members + 1], axis=0, keepdims=True
    )
    scaled = root * (math.sqrt(members - 1.0) * jnp.sqrt(inv))
    return (scaled + mean_weight).astype(jnp.bfloat16)[:, :members]


def analysis_kernel(mine, theirs, ensemble, out, held, result, in_sem, out_sem):
    members, width = held.shape
    fetches, stores, parts = [], [], []
    for i in range(FETCHES):
        part = pl.ds(i * (width // FETCHES), width // FETCHES)
        fetches.append(pltpu.make_async_copy(ensemble.at[:, part], held.at[:, part], in_sem.at[i]))
    for i in range(STORES):
        part = pl.ds(i * (width // STORES), width // STORES)
        parts.append(part)
        stores.append(pltpu.make_async_copy(result.at[:, part], out.at[:, part], out_sem.at[i]))
    for copy in fetches:
        copy.start()
    transform = transform_of(mine[...] + theirs[...])
    share = (1.0 - jnp.sum(transform.astype(jnp.float32), axis=1, keepdims=True)) / members
    left = jnp.concatenate([transform, jnp.ones((SIDE_ROWS, members), jnp.bfloat16)], axis=0)
    for copy in fetches:
        copy.wait()
    for part, copy in zip(parts, stores):
        sums = dot(left, held[:, part])
        mean = share * sums[members : members + 1]
        result[:, part] = (sums[:members] + mean).astype(jnp.bfloat16)
        copy.start()
    for copy in stores:
        copy.wait()


def analysis(grams, ensemble):
    members, width = ensemble.shape
    return pl.pallas_call(
        analysis_kernel,
        in_specs=[pl.BlockSpec(memory_space=pltpu.VMEM)] * len(grams) + [pl.BlockSpec(memory_space=pltpu.HBM)],
        out_specs=pl.BlockSpec(memory_space=pltpu.HBM),
        out_shape=jax.ShapeDtypeStruct((members, width), jnp.bfloat16),
        scratch_shapes=[
            pltpu.VMEM((members, width), jnp.bfloat16),
            pltpu.VMEM((members, width), jnp.bfloat16),
            pltpu.SemaphoreType.DMA((FETCHES,)),
            pltpu.SemaphoreType.DMA((STORES,)),
        ],
        compiler_params=pltpu.CompilerParams(vmem_limit_bytes=VMEM_BYTES),
        name="analysis",
    )(*grams, in_hbm(ensemble))


def local(n_tile, n_lev, ensemble, obs_pert, innovation, obs_rinv, loc_weight, obs_count):
    members = obs_pert.shape[0]
    axes = ("tile", "lev")

    def pairs(partner):
        return [
            (t * n_lev + l, (lambda a, b: a * n_lev + b)(*partner(t, l)))
            for t in range(n_tile)
            for l in range(n_lev)
        ]

    core = pairs(lambda t, l: (t, l ^ 1))
    onward = pairs(lambda t, l: ((t + 1) % n_tile, l ^ (2 * (l & 1))))
    back = pairs(lambda t, l: ((t - 1) % n_tile, l ^ (2 * (l & 1))))
    early = pairs(lambda t, l: (t, l ^ 2 if t % 8 == 0 else l ^ 1))
    late = pairs(lambda t, l: (t, l ^ 1 if t % 8 == 0 else l ^ 2))
    after, right, row_before, row_own = next_gram(
        obs_pert, innovation[None, :], obs_rinv[None, :], loc_weight, obs_count
    )
    before = one_gram(right, row_before)
    after = after + lax.ppermute(after, axes, core)
    after, before, row_own = lax.optimization_barrier((after, before, row_own))
    own = one_gram(right, row_own)
    before = before + lax.ppermute(before, axes, core)
    before, held = lax.optimization_barrier((before, own))
    from_before = lax.ppermute(after, axes, onward)
    from_early = lax.ppermute(own, axes, early)
    from_after = lax.ppermute(before, axes, back)
    from_late = lax.ppermute(held, axes, late)
    first = lax.axis_index("tile") % 8 == 0
    mine = from_before + jnp.where(first, from_early, 0.0) + from_after + jnp.where(first, 0.0, from_late) + own
    return analysis((mine, lax.ppermute(mine, axes, core)), ensemble)


def solution(mesh):
    return jax.shard_map(
        functools.partial(local, mesh.shape["tile"], mesh.shape["lev"]),
        mesh=mesh,
        in_specs=(
            P(None, ("tile", "lev")),
            P(None, ("tile", "lev")),
            P(("tile", "lev")),
            P(("tile", "lev")),
            P(None, ("tile", "lev")),
            P(("tile", "lev")),
        ),
        out_specs=P(None, ("tile", "lev")),
        check_vma=False,
    )
```

```python
import functools
import math

import jax
import jax.numpy as jnp
from jax import lax
from jax.experimental import pallas as pl
from jax.experimental.pallas import tpu as pltpu
from jax.sharding import PartitionSpec as P

NS_STEPS = 10
OBS_CHUNKS = (16384,)
SIDE_ROWS = 16
FETCHES = 4
STORES = 16
VMEM_BYTES = 40 * 1024 * 1024


def in_hbm(array):
    return pltpu.with_memory_space_constraint(array, pltpu.HBM)


def weighted_grams(rows, right):
    members = right.shape[0] - SIDE_ROWS
    left = jnp.concatenate([right[:members] * row for row in rows], axis=0)
    return lax.dot_general(left, right, (((1,), (1,)), ((), ())), preferred_element_type=jnp.float32)


def widened(gram):
    return jnp.concatenate(
        [gram, jnp.zeros((gram.shape[0], 128 - gram.shape[1]), jnp.float32)], axis=1
    )


def next_kernel(
    count, pert, innov, rinv, loc, out, right, first, second, innov_in, rinv_in, loc_in, pert_sem, sem
):
    members, width = pert.shape
    assert sum(OBS_CHUNKS) == width
    parts = [(sum(OBS_CHUNKS[:i]), length) for i, length in enumerate(OBS_CHUNKS)]
    sides = [
        pltpu.make_async_copy(source, target, sem.at[i])
        for i, (source, target) in enumerate(((rinv, rinv_in), (loc, loc_in), (innov, innov_in)))
    ]
    blocks = []
    for i, (start, length) in enumerate(parts):
        part = pl.ds(start, length)
        target = right.at[pl.ds(0, members), part]
        blocks.append(pltpu.make_async_copy(pert.at[:, part], target, pert_sem.at[i]))
    for copy in sides + blocks:
        copy.start()
    for copy in sides:
        copy.wait()
    total = None
    for copy, (start, length) in zip(blocks, parts):
        part = pl.ds(start, length)
        slots = start + lax.broadcasted_iota(jnp.int32, (1, length), 1)
        live = (slots < count[0]).astype(jnp.float32)
        scaled = rinv_in[:, part]
        before, mid, after = [
            (scaled * loc_in[j : j + 1, part] * live).astype(jnp.bfloat16) for j in range(3)
        ]
        first[:, part] = before
        second[:, part] = mid
        right[members:, part] = jnp.broadcast_to(
            innov_in[:, part].astype(jnp.bfloat16), (SIDE_ROWS, length)
        )
        copy.wait()
        gram = weighted_grams((after,), right[:, part])
        total = gram if total is None else total + gram
    out[...] = widened(total)


def next_gram(pert, innov, rinv, loc, count):
    members, width = pert.shape
    return pl.pallas_call(
        next_kernel,
        in_specs=[pl.BlockSpec(memory_space=pltpu.SMEM)]
        + [pl.BlockSpec(memory_space=pltpu.HBM)] * 4,
        out_specs=[pl.BlockSpec(memory_space=pltpu.VMEM)] * 4,
        out_shape=[
            jax.ShapeDtypeStruct((members, 128), jnp.float32),
            jax.ShapeDtypeStruct((members + SIDE_ROWS, width), jnp.bfloat16),
            jax.ShapeDtypeStruct((1, width), jnp.bfloat16),
            jax.ShapeDtypeStruct((1, width), jnp.bfloat16),
        ],
        scratch_shapes=[
            pltpu.VMEM((1, width), jnp.float32),
            pltpu.VMEM((1, width), jnp.float32),
            pltpu.VMEM((3, width), jnp.float32),
            pltpu.SemaphoreType.DMA((len(OBS_CHUNKS),)),
            pltpu.SemaphoreType.DMA((3,)),
        ],
        compiler_params=pltpu.CompilerParams(vmem_limit_bytes=VMEM_BYTES),
        name="next_gram",
    )(count, *(in_hbm(x) for x in (pert, innov, rinv, loc)))


def one_kernel(right, own, out):
    out[...] = widened(weighted_grams((own[...],), right[...]))


def one_gram(right, own):
    members = right.shape[0] - SIDE_ROWS
    width = right.shape[1]
    return pl.pallas_call(
        one_kernel,
        in_specs=[pl.BlockSpec(memory_space=pltpu.VMEM)] * 2,
        out_specs=pl.BlockSpec(memory_space=pltpu.VMEM),
        out_shape=jax.ShapeDtypeStruct((members, 128), jnp.float32),
        compiler_params=pltpu.CompilerParams(vmem_limit_bytes=VMEM_BYTES),
        cost_estimate=pl.CostEstimate(
            flops=2 * members * 128 * width, bytes_accessed=2 * right.size, transcendentals=0
        ),
        name="one_gram",
    )(right, own)


def split(array):
    high = array.astype(jnp.bfloat16)
    rest = array - high.astype(jnp.float32)
    middle = rest.astype(jnp.bfloat16)
    return high, middle, (rest - middle.astype(jnp.float32)).astype(jnp.bfloat16)


def dot(a, b):
    return jnp.dot(a, b, preferred_element_type=jnp.float32)


def product(a, b):
    high, middle, low = a
    below = jnp.zeros((128 - b[0].shape[0], 128), jnp.bfloat16)
    b_high, b_middle, b_low = (jnp.concatenate([part, below], axis=0) for part in b)
    pair = jnp.concatenate([b_high, b_middle], axis=1)
    large = dot(jnp.concatenate([high, middle], axis=1), jnp.concatenate([pair, pair], axis=0))
    small = dot(jnp.concatenate([low, high], axis=1), jnp.concatenate([b_high, b_low], axis=0))
    return (small + large[:, 128:]) + large[:, :128]


def transform_of(total):
    members = total.shape[0]
    rows = lax.broadcasted_iota(jnp.int32, total.shape, 0)
    cols = lax.broadcasted_iota(jnp.int32, total.shape, 1)
    eye = (rows == cols).astype(jnp.float32)
    square = cols < members
    mat = jnp.where(square, total, 0.0) + (members - 1.0) * eye
    proj = jnp.where(cols == members, total, 0.0)
    mat_parts = split(mat)
    squared = product(mat_parts, mat_parts)
    inv = 1.0 / jnp.sqrt(jnp.sum(mat * mat, keepdims=True))
    first = mat * inv
    second = squared * (inv * inv)
    inverse_root = eye + proj
    for triple in range((NS_STEPS - 1) // 3):
        first_parts = split(first)
        if triple:
            second = product(first_parts, first_parts)
        second_parts = split(second)
        third = product(second_parts, first_parts)
        fourth = product(second_parts, second_parts)
        pair = 2.25 * eye - 2.4375 * first + 1.6875 * second - 0.5625 * third + 0.0625 * fourth
        pair_parts = split(pair)
        pair_squared = split(product(pair_parts, pair_parts))
        first_pair = product(first_parts, pair_parts)
        second_pair = split(product(second_parts, pair_parts))
        factor = split(1.5 * pair - 0.5 * product(pair_squared, split(first_pair)))
        scaled = split(1.5 * first_pair - 0.5 * product(second_pair, pair_squared))
        first = product(scaled, factor)
        inverse_root = product(factor, split(inverse_root))
    inverse_root = product(split(1.5 * eye - 0.5 * first), split(inverse_root))
    root = jnp.where(square, inverse_root, 0.0)
    mean_weight = inv * jnp.sum(
        root * inverse_root[:, members : members + 1], axis=0, keepdims=True
    )
    scaled = root * (math.sqrt(members - 1.0) * jnp.sqrt(inv))
    return (scaled + mean_weight).astype(jnp.bfloat16)[:, :members]


def analysis_kernel(mine, theirs, ensemble, out, held, result, in_sem, out_sem):
    members, width = held.shape
    fetches, stores, parts = [], [], []
    for i in range(FETCHES):
        part = pl.ds(i * (width // FETCHES), width // FETCHES)
        fetches.append(pltpu.make_async_copy(ensemble.at[:, part], held.at[:, part], in_sem.at[i]))
    for i in range(STORES):
        part = pl.ds(i * (width // STORES), width // STORES)
        parts.append(part)
        stores.append(pltpu.make_async_copy(result.at[:, part], out.at[:, part], out_sem.at[i]))
    for copy in fetches:
        copy.start()
    transform = transform_of(mine[...] + theirs[...])
    share = (1.0 - jnp.sum(transform.astype(jnp.float32), axis=1, keepdims=True)) / members
    left = jnp.concatenate([transform, jnp.ones((SIDE_ROWS, members), jnp.bfloat16)], axis=0)
    for copy in fetches:
        copy.wait()
    for part, copy in zip(parts, stores):
        sums = dot(left, held[:, part])
        mean = share * sums[members : members + 1]
        result[:, part] = (sums[:members] + mean).astype(jnp.bfloat16)
        copy.start()
    for copy in stores:
        copy.wait()


def analysis(grams, ensemble):
    members, width = ensemble.shape
    return pl.pallas_call(
        analysis_kernel,
        in_specs=[pl.BlockSpec(memory_space=pltpu.VMEM)] * len(grams) + [pl.BlockSpec(memory_space=pltpu.HBM)],
        out_specs=pl.BlockSpec(memory_space=pltpu.HBM),
        out_shape=jax.ShapeDtypeStruct((members, width), jnp.bfloat16),
        scratch_shapes=[
            pltpu.VMEM((members, width), jnp.bfloat16),
            pltpu.VMEM((members, width), jnp.bfloat16),
            pltpu.SemaphoreType.DMA((FETCHES,)),
            pltpu.SemaphoreType.DMA((STORES,)),
        ],
        compiler_params=pltpu.CompilerParams(vmem_limit_bytes=VMEM_BYTES),
        name="analysis",
    )(*grams, in_hbm(ensemble))


def local(n_tile, n_lev, ensemble, obs_pert, innovation, obs_rinv, loc_weight, obs_count):
    members = obs_pert.shape[0]
    axes = ("tile", "lev")

    def pairs(partner):
        return [
            (t * n_lev + l, (lambda a, b: a * n_lev + b)(*partner(t, l)))
            for t in range(n_tile)
            for l in range(n_lev)
        ]

    core = pairs(lambda t, l: (t, l ^ 1))
    onward = pairs(lambda t, l: ((t + 1) % n_tile, l ^ (2 * (l & 1))))
    back = pairs(lambda t, l: ((t - 1) % n_tile, l ^ (2 * (l & 1))))
    early = pairs(lambda t, l: (t, l ^ 2 if t % 2 == 0 else l ^ 1))
    late = pairs(lambda t, l: (t, l ^ 1 if t % 2 == 0 else l ^ 2))
    after, right, row_before, row_own = next_gram(
        obs_pert, innovation[None, :], obs_rinv[None, :], loc_weight, obs_count
    )
    before = one_gram(right, row_before)
    after = after + lax.ppermute(after, axes, core)
    after, before, row_own = lax.optimization_barrier((after, before, row_own))
    own = one_gram(right, row_own)
    before = before + lax.ppermute(before, axes, core)
    before, held = lax.optimization_barrier((before, own))
    from_before = lax.ppermute(after, axes, onward)
    from_early = lax.ppermute(own, axes, early)
    from_after = lax.ppermute(before, axes, back)
    from_late = lax.ppermute(held, axes, late)
    first = lax.axis_index("tile") % 2 == 0
    mine = from_before + jnp.where(first, from_early, 0.0) + from_after + jnp.where(first, 0.0, from_late) + own
    return analysis((mine, lax.ppermute(mine, axes, core)), ensemble)


def solution(mesh):
    return jax.shard_map(
        functools.partial(local, mesh.shape["tile"], mesh.shape["lev"]),
        mesh=mesh,
        in_specs=(
            P(None, ("tile", "lev")),
            P(None, ("tile", "lev")),
            P(("tile", "lev")),
            P(("tile", "lev")),
            P(None, ("tile", "lev")),
            P(("tile", "lev")),
        ),
        out_specs=P(None, ("tile", "lev")),
        check_vma=False,
    )
```
